32 devices in a mesh: group: 2 (over y), expert: 4 (over z), head: 4 (over x, core).
Axes of the slice: x: 2, y: 2, z: 4, core: 2. Of those that a mesh axis runs over, the one named last changes fastest.
Arguments:
- q_latent: bfloat16 [512, 32768], P(('group', 'expert'), 'head'), parts along dimension 0, may hold values from -100 to 100
- q_rope: bfloat16 [512, 4096], P(('group', 'expert'), 'head'), parts along dimension 0, may hold values from -100 to 100
- prefix_latent: bfloat16 [128, 512], P(('group', 'expert')), parts along dimension 0, may hold values from -6 to 6
- prefix_rope: bfloat16 [128, 64], P(('group', 'expert')), parts along dimension 0, may hold values from -6 to 6
- span_latent: bfloat16 [512, 512], P(('group', 'expert')), parts along dimension 0, may hold values from -6 to 6
- span_rope: bfloat16 [512, 64], P(('group', 'expert')), parts along dimension 0, may hold values from -6 to 6
- prefix_len: int32 [2], P('group'), parts along dimension 0, may hold values from 16 to 64
- moe_input: bfloat16 [512, 7168], P(('group', 'expert'), 'head'), parts along dimension 0, may hold values from -6 to 6
- routes: int32 [512, 2], P(('group', 'expert')), parts along dimension 0, may hold values from 0 to 3, all different within a row; in each aligned block of 64 rows (0 to 63, 64 to 127, ...) at most 36 rows name the same one
- owners: int32 [8], P('group'), parts along dimension 0, may hold values from 0 to 3, each once
- gate_weight: bfloat16 [4, 7168, 1024], P('expert', None, 'head'), may hold values from -0.0625 to 0.0625
- up_weight: bfloat16 [4, 7168, 1024], P('expert', None, 'head'), may hold values from -0.0625 to 0.0625
Outputs:
- attended: bfloat16 [512, 32768], P(('group', 'expert'), 'head'), parts along dimension 0
- expert_hidden: bfloat16 [8, 144, 1024], P(('group', 'expert'), None, 'head'), parts along dimension 0
- migrated_latent: bfloat16 [640, 512], P(('group', 'expert')), parts along dimension 0
- migrated_rope: bfloat16 [640, 64], P(('group', 'expert')), parts along dimension 0
The draws below stay inside these ranges and needn't reach their ends.
There are 2 independent parts, one for each index of `group`. The reference program is written for one: setup_inputs(seed, part) draws one part's arguments, and reference() takes and returns one part's arrays. A program takes and returns all parts, laid end to end along the dimension named above; an argument that names none is the same for every part. Nothing has to cross between parts.
Inputs may be any that keep to these rules, and one draw needn't show every extreme that they name: `routes`: among the 64 rows of one device no expert is named by more than 36 rows, a bound that some block reaches. `owners`: A permutation of 0 to 3.
All inputs are finite; a program needn't handle non-finite values.
Results may differ from the reference program's by a relative error of at most 0.0049.
Values may be sent and summed in bfloat16 or wider, within the bound.
A program may use at most 128 MiB of HBM per device.

```python
import math
import jax
import jax.numpy as jnp
import numpy as np
from jax import lax

D = 7168
LATENT = 512
ROPE = 64
HEADS = 64
FF_WIN = 1024
TOK_DEV = 64
PRE_DEV = 16
TOKENS = 256
PREFIX = 64
EXPERTS = 4
TOPK = 2
CAP = 36
N_EXPERT = 4


def cache_tables(key):
    pre_lat = jnp.clip(jax.random.normal(jax.random.fold_in(key, 101), (PREFIX, LATENT), jnp.float32), -6.0, 6.0)
    pre_rot = jnp.clip(jax.random.normal(jax.random.fold_in(key, 102), (PREFIX, ROPE), jnp.float32), -6.0, 6.0)
    chk_lat = jnp.clip(jax.random.normal(jax.random.fold_in(key, 103), (TOKENS, LATENT), jnp.float32), -6.0, 6.0)
    chk_rot = jnp.clip(jax.random.normal(jax.random.fold_in(key, 104), (TOKENS, ROPE), jnp.float32), -6.0, 6.0)
    return (pre_lat, pre_rot, chk_lat, chk_rot)


def draw_prefix_latent(key, part):
    tables = cache_tables(key)
    return tables[0].astype(jnp.bfloat16)


def draw_prefix_rope(key, part):
    tables = cache_tables(key)
    return tables[1].astype(jnp.bfloat16)


def draw_span_latent(key, part):
    tables = cache_tables(key)
    return tables[2].astype(jnp.bfloat16)


def draw_span_rope(key, part):
    tables = cache_tables(key)
    return tables[3].astype(jnp.bfloat16)


def draw_q_latent(key, part):
    key = jax.random.fold_in(key, 5)
    queries = jnp.clip(jax.random.normal(key, (TOKENS, HEADS, LATENT), jnp.float32), -6.0, 6.0)
    return queries.reshape(TOKENS, HEADS * LATENT).astype(jnp.bfloat16)


def draw_q_rope(key, part):
    key = jax.random.fold_in(key, 6)
    queries = jnp.clip(jax.random.normal(key, (TOKENS, HEADS, ROPE), jnp.float32), -6.0, 6.0)
    return queries.reshape(TOKENS, HEADS * ROPE).astype(jnp.bfloat16)


def shard_levels(key, dims, split, low, high):
    def one(axis_at, shards_of):
        heights = jax.random.uniform(jax.random.fold_in(jax.random.fold_in(key, 6), axis_at), (shards_of,), jnp.float32, low / len(split), high / len(split))
        return jnp.repeat(jnp.exp(heights), dims[axis_at] // shards_of).reshape((-1,) + (1,) * (len(dims) - axis_at - 1))

    gain = one(*split[0])
    for cut in split[1:]:
        gain = gain * one(*cut)
    return gain


def deal_out(own_key, own, number, rows, count, top, bound, slope):
    order = jax.random.permutation(own_key, count)
    crowded, usual = load_shares(count, rows * top, bound, slope, True), load_shares(count, rows * top, bound, slope, False)
    places = jnp.arange(count)

    def named(tallies, offset_by):
        used = int((tallies > 0).sum())
        fixed = max(1, used // 4)
        moved = fixed + (places - fixed + offset_by * (used - fixed)) % max(1, count - fixed)
        return jnp.zeros((count,), jnp.int32).at[order[jnp.where(places < fixed, places, moved)]].set(jnp.asarray(tallies, jnp.int32))

    tallies = jnp.where(number % 4 == 0, named(crowded, number // 4), named(usual, number - number // 4 - 1))
    mixed = jax.random.permutation(jax.random.fold_in(own, 3), count)
    source_of, sink = mixed[0:count // 2 * 2:2], mixed[1:count // 2 * 2:2]
    room = jnp.minimum(tallies[source_of] - 1, bound - tallies[sink]) // 2
    room = jnp.where((source_of == order[0]) | (sink == order[0]) | (tallies[sink] == 0), 0, jnp.maximum(room, 0))
    moved = jax.random.randint(jax.random.fold_in(own, 4), (count // 2,), 0, 1 << 20) % (room + 1)
    tallies = tallies.at[source_of].add(-moved).at[sink].add(moved)
    items = jnp.searchsorted(jnp.cumsum(tallies), jnp.arange(rows * top), side="right").astype(jnp.int32)
    listing = items.reshape(top, rows).T
    listing = listing[jax.random.permutation(jax.random.fold_in(own, 1), rows)]
    offset_by = jax.random.randint(jax.random.fold_in(own, 2), (rows, 1), 0, top)
    return jnp.take_along_axis(listing, (jnp.arange(top)[None, :] + offset_by) % top, axis=1)


def load_shares(count, total, most, lean, full):
    portions = [(1 << 20) // math.isqrt(grade ** lean) + 1 for grade in range(1, count + 1)]
    largest = most if full else min(most, max(-(-total // count), total * portions[0] // sum(portions)))
    least = 1 if total - largest >= count - 1 else 0
    holding, surplus = [largest] + [least] * (count - 1), total - largest - least * (count - 1)
    while surplus > 0:
        free = [i for i in range(1, count) if holding[i] < largest] or [i for i in range(1, count) if holding[i] < most]
        whole, budget = sum([portions[i] for i in free]), surplus
        for i in free:
            more = min(most - holding[i], max(1, budget * portions[i] // whole), surplus)
            holding[i] = holding[i] + more
            surplus = surplus - more
    return np.array(holding)


def bell_draw(own_key, dims, width, bound, pieces=(), kind=jnp.bfloat16):
    result = jax.random.normal(own_key, dims, jnp.float32) * width
    if len(pieces) > 0:
        result = shard_levels(own_key, dims, pieces, -0.22, 0.18) * result
    return jnp.clip(result, min=-bound, max=bound).astype(kind)


def setup_inputs(seed: int = 0, part: int = 0) -> dict:
    keys = jax.random.split(jax.random.key(seed), 13)
    own_keys = jax.random.split(jax.random.fold_in(keys[12], part), 13)
    q_latent = draw_q_latent(jax.random.fold_in(jax.random.fold_in(keys[12], part), 71), part)
    q_rope = draw_q_rope(jax.random.fold_in(jax.random.fold_in(keys[12], part), 71), part)
    prefix_latent = draw_prefix_latent(jax.random.fold_in(jax.random.fold_in(keys[12], part), 71), part)
    prefix_rope = draw_prefix_rope(jax.random.fold_in(jax.random.fold_in(keys[12], part), 71), part)
    span_latent = draw_span_latent(jax.random.fold_in(jax.random.fold_in(keys[12], part), 71), part)
    span_rope = draw_span_rope(jax.random.fold_in(jax.random.fold_in(keys[12], part), 71), part)
    prefix_len = jax.random.randint(own_keys[6], (1,), PREFIX // 4, PREFIX + 1).astype(jnp.int32)
    moe_input = bell_draw(own_keys[7], (TOKENS, D), 1.0, 6.0, ((0, 4), (1, 4)))
    routes_keys = jax.random.split(jax.random.fold_in(own_keys[8], 1), TOKENS // TOK_DEV)
    routes_turns = jax.random.permutation(jax.random.fold_in(own_keys[8], 3), TOKENS // TOK_DEV)
    routes = jax.vmap(lambda own, number: deal_out(jax.random.fold_in(own_keys[8], 2), own, number, TOK_DEV, EXPERTS, TOPK, CAP, 2))(routes_keys, routes_turns).reshape((TOKENS, TOPK))
    owners = jax.random.permutation(own_keys[9], EXPERTS).astype(jnp.int32)
    gate_weight = bell_draw(keys[10], (EXPERTS, D, FF_WIN), D ** -0.5, 0.0625, ((0, 4), (2, 4)))
    up_weight = bell_draw(keys[11], (EXPERTS, D, FF_WIN), D ** -0.5, 0.0625, ((0, 4), (2, 4)))
    return dict(q_latent=q_latent, q_rope=q_rope, prefix_latent=prefix_latent, prefix_rope=prefix_rope, span_latent=span_latent, span_rope=span_rope, prefix_len=prefix_len, moe_input=moe_input, routes=routes, owners=owners, gate_weight=gate_weight, up_weight=up_weight)


softmax_scale = 192.0 ** -0.5


def reference(q_latent, q_rope, prefix_latent, prefix_rope, span_latent, span_rope, prefix_len, moe_input, routes, owners, gate_weight, up_weight):
    limit = prefix_len[0]
    prefix_alive = jnp.arange(PREFIX, dtype=jnp.int32) < limit
    kept_latent = jnp.where(prefix_alive[:, None], prefix_latent, jnp.zeros_like(prefix_latent))
    kept_rope = jnp.where(prefix_alive[:, None], prefix_rope, jnp.zeros_like(prefix_rope))
    keys_latent = jnp.concatenate([kept_latent, span_latent], axis=0)
    keys_rope = jnp.concatenate([kept_rope, span_rope], axis=0)
    columns = jnp.arange(PREFIX + TOKENS, dtype=jnp.int32)
    query_pos = jnp.arange(TOKENS, dtype=jnp.int32)
    allowed = jnp.where(columns[None, :] < PREFIX, (columns < limit)[None, :], (columns - PREFIX)[None, :] <= query_pos[:, None])
    lat_heads = q_latent.reshape(TOKENS, HEADS, LATENT).transpose(1, 0, 2)
    rope_heads = q_rope.reshape(TOKENS, HEADS, ROPE).transpose(1, 0, 2)

    def one_head(pair):
        query_lat, query_rot = pair
        scores = (jnp.dot(query_lat, keys_latent.T, preferred_element_type=jnp.float32) + jnp.dot(query_rot, keys_rope.T, preferred_element_type=jnp.float32)) * softmax_scale
        masked = jnp.where(allowed, scores, -1e30)
        peak = jnp.max(masked, axis=1, keepdims=True)
        weights = jnp.where(allowed, jnp.exp(masked - peak), 0.0)
        total = jnp.sum(weights, axis=1, keepdims=True)
        weights_round = weights.astype(jnp.bfloat16)
        mixed = jnp.dot(weights_round, keys_latent, preferred_element_type=jnp.float32)
        return (mixed / total).astype(jnp.bfloat16)

    attended = lax.map(one_head, (lat_heads, rope_heads)).transpose(1, 0, 2).reshape(TOKENS, HEADS * LATENT)

    block_lat = jnp.concatenate([kept_latent.reshape(N_EXPERT, PRE_DEV, LATENT), span_latent.reshape(N_EXPERT, TOK_DEV, LATENT)], axis=1)
    block_rot = jnp.concatenate([kept_rope.reshape(N_EXPERT, PRE_DEV, ROPE), span_rope.reshape(N_EXPERT, TOK_DEV, ROPE)], axis=1)
    migrated_latent = jnp.zeros_like(block_lat).at[owners].set(block_lat).reshape(N_EXPERT * (PRE_DEV + TOK_DEV), LATENT)
    migrated_rope = jnp.zeros_like(block_rot).at[owners].set(block_rot).reshape(N_EXPERT * (PRE_DEV + TOK_DEV), ROPE)

    expert_ids = jnp.arange(EXPERTS, dtype=jnp.int32)
    routed = jnp.any(routes[:, :, None] == expert_ids[None, None, :], axis=1).astype(jnp.int32).reshape(N_EXPERT, TOK_DEV, EXPERTS)
    slot_rank = jnp.cumsum(routed, axis=1) - 1
    tokens_wide = moe_input.reshape(N_EXPERT, TOK_DEV, D).astype(jnp.float32)
    slot_ids = jnp.arange(CAP, dtype=jnp.int32)

    def one_expert(triple):
        expert, w_gate, w_up = triple
        chosen = routed[:, :, expert]
        ranks = slot_rank[:, :, expert]
        dispatch = ((chosen[:, None, :] == 1) & (ranks[:, None, :] == slot_ids[None, :, None])).astype(jnp.float32)
        expert_rows = jnp.einsum('sct,std->scd', dispatch, tokens_wide, precision=lax.Precision.HIGHEST).astype(jnp.bfloat16).reshape(N_EXPERT * CAP, D)
        gated = jnp.dot(expert_rows, w_gate, preferred_element_type=jnp.float32)
        upward = jnp.dot(expert_rows, w_up, preferred_element_type=jnp.float32)
        return (jax.nn.silu(gated) * upward).astype(jnp.bfloat16)

    expert_hidden = lax.map(one_expert, (expert_ids, gate_weight, up_weight))
    return attended, expert_hidden, migrated_latent, migrated_rope
```

```python
import functools

import jax
import jax.numpy as jnp
from jax import lax
from jax.experimental import pallas as pl
from jax.experimental.pallas import tpu as pltpu
from jax.sharding import PartitionSpec as P

SOFTMAX_SCALE = 192.0 ** (-0.5)
MESH = pl.DeviceIdType.MESH
NT = (((1,), (1,)), ((), ()))


def each(count, step):
    if count <= 4:
        for i in range(count):
            step(i)
    else:
        def one(i, carry):
            step(i)
            return carry
        lax.fori_loop(0, count, one, 0)


def each_from(first, count, step):
    each(count - first, lambda i: step(i + first))


class Plan:
    def __init__(self, n, heads_axis, tok, pre, lat, rope, heads, width, top, hidden):
        self.n, self.nh, self.nx = n, heads_axis, heads_axis // 2
        self.tok, self.pre, self.lat, self.rope, self.heads = tok, pre, lat, rope, heads
        self.block = tok + pre
        self.keys = n * self.block
        self.kw = lat + 2 * rope
        self.width, self.top, self.hidden = width, top, hidden
        self.cap = min(tok, max(2, 9 * tok * top // (8 * n)))
        self.cw = 256 if width % 256 == 0 else 128
        self.chunks = width // self.cw
        self.main = self.cap // 16 * 16
        self.tail = self.cap - self.main
        self.parts = 16 // self.tail if self.tail else 0
        self.per_part = -(-self.chunks // self.parts) if self.tail else 0
        self.slot_rows = self.chunks * self.main + 16 * self.per_part
        first = -(-(self.kw // 128) // 2) * 128
        self.cols = (pl.ds(0, first), pl.ds(first, self.kw - first))


def kernel(
    p,
    limit_ref, owners_ref, routes_ref, feat_ref, prelat_ref, prerope_ref, spanlat_ref, spanrope_ref,
    qlat_hbm, qrope_hbm, gate_hbm, up_hbm,
    att_ref, hidden_ref, miglat_ref, migrope_ref,
    qlat, qrope, gate, up, kv, slots, outgoing, bias, assembled,
    local_sem, kvz_s, kvz_r, kvc_s, kvc_r, sz_s, sz_r, sx_s, sx_r, sc_s, sc_r,
):
    n, nx = p.n, p.nx
    me = lax.axis_index("expert")
    head = lax.axis_index("head")
    core = lax.rem(head, 2)
    xpos = lax.div(head, 2)
    partner = head + 1 - 2 * core

    def z_to(k):
        return lax.rem(me - k + n, n)

    def z_from(k):
        return lax.rem(me + k, n)

    def x_to(j):
        return lax.rem(xpos - j + nx, nx) * 2 + core

    def x_from(j):
        return lax.rem(xpos + j, nx) * 2 + core

    barrier = pltpu.get_barrier_semaphore()
    each_from(1, n, lambda k: pl.semaphore_signal(
        barrier, inc=1, device_id={"expert": z_to(k)}, device_id_type=MESH))
    each_from(1, nx, lambda j: pl.semaphore_signal(
        barrier, inc=1, device_id={"head": x_to(j)}, device_id_type=MESH))
    pl.semaphore_signal(barrier, inc=1, device_id={"head": partner}, device_id_type=MESH)

    loads = [
        pltpu.make_async_copy(src, dst, local_sem.at[i])
        for i, (src, dst) in enumerate(
            ((qlat_hbm, qlat), (qrope_hbm, qrope), (gate_hbm.at[0], gate), (up_hbm.at[0], up)))
    ]
    for load in loads:
        load.start()

    limit = limit_ref[0]
    prefix_pos = me * p.pre + lax.broadcasted_iota(jnp.int32, (p.pre, 1), 0)
    kept = prefix_pos < limit
    zero_pad = jnp.zeros((p.pre, p.rope), jnp.float32)
    kv[me, 0:p.pre, 0:p.lat] = jnp.where(
        kept, prelat_ref[...].astype(jnp.float32), 0.0).astype(jnp.bfloat16)
    kv[me, p.pre:p.block, 0:p.lat] = spanlat_ref[...]
    kv[me, 0:p.pre, p.lat:p.kw] = jnp.concatenate(
        [jnp.where(kept, prerope_ref[...].astype(jnp.float32), 0.0), zero_pad], axis=1
    ).astype(jnp.bfloat16)
    kv[me, p.pre:p.block, p.lat:p.kw] = jnp.concatenate(
        [spanrope_ref[...], jnp.zeros((p.tok, p.rope), jnp.bfloat16)], axis=1)

    feats = feat_ref[...]
    older = (lax.broadcasted_iota(jnp.int32, (p.tok, p.tok), 0)
             <= lax.broadcasted_iota(jnp.int32, (p.tok, p.tok), 1))
    older = older.astype(jnp.float32).astype(jnp.bfloat16)
    sel_rows = p.main + (16 if p.tail else 0)
    row = lax.broadcasted_iota(jnp.int32, (sel_rows, p.tok), 0)
    slot_id = row
    if p.tail:
        for q in range(1, p.parts):
            slot_id = slot_id - jnp.where(row >= p.main + q * p.tail, p.tail, 0)
    slot_id = slot_id.astype(jnp.float32)

    def slot_values(expert, put):
        named = jnp.zeros((1, p.tok), jnp.float32)
        for t in range(p.top):
            named = jnp.maximum(named, (routes_ref[t:t + 1, :] == expert).astype(jnp.float32))
        named8 = jnp.broadcast_to(named, (16, p.tok))
        rank = jnp.dot(named8.astype(jnp.bfloat16), older, preferred_element_type=jnp.float32) - 1.0
        rank = jnp.where(named8 > 0.5, rank, -1.0)[0:1, :]
        chosen = (rank == slot_id).astype(jnp.float32).astype(jnp.bfloat16)
        picked = jnp.dot(chosen, feats, preferred_element_type=jnp.float32)
        for c in range(p.chunks):
            put(c * p.main, p.main,
                picked[0:p.main, c * p.cw:(c + 1) * p.cw].astype(jnp.bfloat16))
        if p.tail:
            trow = lax.broadcasted_iota(jnp.int32, (16, p.cw), 0)
            for part in range(p.per_part):
                value = jnp.zeros((16, p.cw), jnp.float32)
                for q in range(p.parts):
                    c = q * p.per_part + part
                    if c < p.chunks:
                        inside = (trow >= q * p.tail) & (trow < (q + 1) * p.tail)
                        value = jnp.where(
                            inside, picked[p.main:sel_rows, c * p.cw:(c + 1) * p.cw], value)
                put(p.chunks * p.main + 16 * part, 16, value.astype(jnp.bfloat16))

    def fill(k):
        def put(at, rows, value):
            outgoing[k, at:at + rows, :] = value
        slot_values(z_to(k), put)

    def fill_own():
        def put(at, rows, value):
            slots[head, me, at:at + rows, :] = value
        slot_values(me, put)

    def kv_z(k, c):
        return pltpu.make_async_remote_copy(
            src_ref=kv.at[me, :, p.cols[c]], dst_ref=kv.at[me, :, p.cols[c]],
            send_sem=kvz_s.at[k], recv_sem=kvz_r.at[k],
            device_id={"expert": z_to(k)}, device_id_type=MESH)

    def kv_z_in(k, c):
        src = z_from(k)
        return pltpu.make_async_remote_copy(
            src_ref=kv.at[src, :, p.cols[c]], dst_ref=kv.at[src, :, p.cols[c]],
            send_sem=kvz_s.at[k], recv_sem=kvz_r.at[k],
            device_id={"expert": z_to(k)}, device_id_type=MESH)

    def kv_c(k, c):
        src = z_from(k)
        return pltpu.make_async_remote_copy(
            src_ref=kv.at[src, :, p.cols[c]], dst_ref=kv.at[src, :, p.cols[c]],
            send_sem=kvc_s.at[k], recv_sem=kvc_r.at[k],
            device_id={"head": partner}, device_id_type=MESH)

    def slot_z(k):
        return pltpu.make_async_remote_copy(
            src_ref=outgoing.at[k], dst_ref=slots.at[head, me],
            send_sem=sz_s.at[k], recv_sem=sz_r.at[k],
            device_id={"expert": z_to(k)}, device_id_type=MESH)

    def slot_z_in(k):
        return pltpu.make_async_remote_copy(
            src_ref=outgoing.at[k], dst_ref=slots.at[head, z_from(k)],
            send_sem=sz_s.at[k], recv_sem=sz_r.at[k],
            device_id={"expert": z_to(k)}, device_id_type=MESH)

    def slot_x(j, k, whose):
        ref = slots.at[whose, z_from(k)]
        return pltpu.make_async_remote_copy(
            src_ref=ref, dst_ref=ref, send_sem=sx_s.at[j, k], recv_sem=sx_r.at[j, k],
            device_id={"head": x_to(j)}, device_id_type=MESH)

    def slot_c(j, k, whose):
        ref = slots.at[whose, z_from(k)]
        return pltpu.make_async_remote_copy(
            src_ref=ref, dst_ref=ref, send_sem=sc_s.at[j, k], recv_sem=sc_r.at[j, k],
            device_id={"head": partner}, device_id_type=MESH)

    def by_core(step):
        for c in (0, 1):
            pl.when(core == c)(functools.partial(step, c))

    def forward_own(k):
        each_from(1, nx, lambda j: slot_x(j, k, head).start())
        slot_c(0, k, head).start()

    def forward_x(k):
        def one(j):
            slot_x(j, k, x_from(j)).wait_recv()
            slot_c(j, k, x_from(j)).start()
        each_from(1, nx, one)

    each_from(1, n, fill)
    fill_own()

    pl.semaphore_wait(barrier, n - 1 + nx - 1 + 1)

    by_core(lambda c: each_from(1, n, lambda k: kv_z(k, c).start()))
    each_from(1, n, lambda k: slot_z(k).start())
    forward_own(0)

    col = lax.broadcasted_iota(jnp.int32, (p.tok, p.keys), 1).astype(jnp.float32)
    query = (me * p.tok + lax.broadcasted_iota(jnp.int32, (p.tok, p.keys), 0)).astype(jnp.float32)
    source = jnp.floor((col + 0.5) * (1.0 / p.block))
    within = col - source * p.block
    in_prefix = within < p.pre
    reach = jnp.where(in_prefix, limit.astype(jnp.float32) - 1.0, query)
    place = jnp.where(in_prefix, source * p.pre + within, source * p.tok + within - p.pre)
    bias[...] = jnp.where(place <= reach, 0.0, -1e30)

    def kv_forward(c):
        def one(k):
            kv_z_in(k, c).wait_recv()
            kv_c(k, c).start()
        each_from(1, n, one)

    def kv_take(c):
        each_from(1, n, lambda k: kv_c(k, 1 - c).wait_recv())

    by_core(kv_forward)
    by_core(kv_take)
    loads[0].wait()
    loads[1].wait()

    group = 4 if p.heads % 4 == 0 else 2
    pairs = group // 2

    def attend(g):
        keys = kv[...].reshape(p.keys, p.kw)
        values = keys[:, 0:p.lat]
        rope_even = keys[:, p.lat:p.kw]
        rope_odd = jnp.concatenate([rope_even[:, p.rope:], rope_even[:, :p.rope]], axis=1)
        order = list(range(0, group, 2)) + list(range(1, group, 2))

        def lat_at(h):
            return pl.ds(pl.multiple_of((g * group + h) * p.lat, 128), p.lat)

        q_lat = jnp.concatenate([qlat[:, lat_at(h)] for h in order], axis=0)
        q_rot = jnp.concatenate(
            [qrope[:, pl.ds(pl.multiple_of((g * pairs + i) * 2 * p.rope, 128), 2 * p.rope)]
             for i in range(pairs)], axis=0)
        scores = lax.dot_general(q_lat, values, NT, preferred_element_type=jnp.float32)
        rot = jnp.concatenate(
            [lax.dot_general(q_rot, rope_even, NT, preferred_element_type=jnp.float32),
             lax.dot_general(q_rot, rope_odd, NT, preferred_element_type=jnp.float32)], axis=0)
        shown = (scores + rot) * SOFTMAX_SCALE + jnp.concatenate([bias[...]] * group, axis=0)
        weights = jnp.exp(shown - jnp.max(shown, axis=1, keepdims=True))
        total = jnp.sum(weights, axis=1, keepdims=True)
        mixed = jnp.dot(weights.astype(jnp.bfloat16), values, preferred_element_type=jnp.float32)
        result = (mixed / total).astype(jnp.bfloat16)
        for i, h in enumerate(order):
            att_ref[:, lat_at(h)] = result[i * p.tok:(i + 1) * p.tok, :]

    steps = p.heads // group
    done = 0
    for k in range(1, n) if n <= 4 else []:
        slot_z_in(k).wait_recv()
        forward_own(k)
        forward_x(k - 1)
        upto = steps * k // (n - 1)
        if upto > done:
            lax.fori_loop(done, upto, lambda g, carry: (attend(g), carry)[1], 0)
        done = upto
    if n > 4:
        def many(k):
            slot_z_in(k).wait_recv()
            forward_own(k)
            forward_x(k - 1)
        each_from(1, n, many)
        lax.fori_loop(0, steps, lambda g, carry: (attend(g), carry)[1], 0)

    mine = jnp.int32(0)
    for s in range(n):
        mine = jnp.where(owners_ref[s] == me, s, mine)
    block = kv[mine]
    miglat_ref[...] = block[:, 0:p.lat]
    migrope_ref[...] = block[:, p.lat:p.lat + p.rope]

    loads[2].wait()
    loads[3].wait()
    rows_main, rows_tail = n * p.main, 16 * n if p.tail else 0
    tail_row = lax.broadcasted_iota(jnp.int32, (n, 16, p.cw), 1)

    def expert_part(which, totals):
        gated, upward = totals
        for c in range(p.chunks):
            lhs = slots[which, :, c * p.main:(c + 1) * p.main, :].reshape(rows_main, p.cw)
            if p.tail:
                q, part = c // p.per_part, c % p.per_part
                at = p.chunks * p.main + 16 * part
                extra = slots[which, :, at:at + 16, :].astype(jnp.float32)
                inside = (tail_row >= q * p.tail) & (tail_row < (q + 1) * p.tail)
                extra = jnp.where(inside, extra, 0.0).astype(jnp.bfloat16)
                lhs = jnp.concatenate([lhs, extra.reshape(rows_tail, p.cw)], axis=0)
            at = pl.ds(pl.multiple_of(which * p.width + c * p.cw, 128), p.cw)
            gated = gated + jnp.dot(lhs, gate[at, :], preferred_element_type=jnp.float32)
            upward = upward + jnp.dot(lhs, up[at, :], preferred_element_type=jnp.float32)
        return gated, upward

    zero = jnp.zeros((rows_main + rows_tail, p.hidden), jnp.float32)
    totals = expert_part(head, (zero, zero))
    each(n, lambda k: slot_c(0, k, partner).wait_recv())
    totals = expert_part(partner, totals)
    forward_x(n - 1)
    for j in range(1, nx):
        totals = expert_part(x_from(j), totals)
    for j in range(1, nx):
        whose = x_from(j) + 1 - 2 * core
        each(n, lambda k: slot_c(j, k, whose).wait_recv())
        totals = expert_part(whose, totals)
    gated, upward = totals

    def finish(g, u):
        return g / (1.0 + jnp.exp(-g)) * u

    for s in range(n):
        at = slice(s * p.main, (s + 1) * p.main)
        assembled[s * p.cap:s * p.cap + p.main, :] = finish(gated[at, :], upward[at, :])
        if p.tail:
            g = jnp.zeros((p.tail, p.hidden), jnp.float32)
            u = g
            for q in range(p.parts):
                at = rows_main + 16 * s + q * p.tail
                g = g + gated[at:at + p.tail, :]
                u = u + upward[at:at + p.tail, :]
            assembled[s * p.cap + p.main:(s + 1) * p.cap, :] = finish(g, u)
    hidden_ref[0] = assembled[...].astype(jnp.bfloat16)

    by_core(lambda c: each_from(1, n, lambda k: kv_z(k, c).wait_send()))
    by_core(lambda c: each_from(1, n, lambda k: kv_c(k, c).wait_send()))
    each_from(1, n, lambda k: slot_z(k).wait_send())

    def sent(k):
        each_from(1, nx, lambda j: slot_x(j, k, head).wait_send())
        slot_c(0, k, head).wait_send()
        each_from(1, nx, lambda j: slot_c(j, k, x_from(j)).wait_send())
    each(n, sent)


def body(
    q_latent, q_rope, prefix_latent, prefix_rope, span_latent, span_rope,
    prefix_len, moe_input, routes, owners, gate_weight, up_weight,
):
    n = lax.axis_size("expert")
    nh = lax.axis_size("head")
    rope = span_rope.shape[1]
    p = Plan(
        n, nh, span_latent.shape[0], prefix_latent.shape[0], span_latent.shape[1], rope,
        q_rope.shape[1] // rope, moe_input.shape[1], routes.shape[1], gate_weight.shape[2])
    bf16, f32 = jnp.bfloat16, jnp.float32
    vmem = pl.BlockSpec(memory_space=pltpu.VMEM)
    smem = pl.BlockSpec(memory_space=pltpu.SMEM)
    hbm = pl.BlockSpec(memory_space=pl.ANY)
    dma = pltpu.SemaphoreType.DMA
    return pl.pallas_call(
        functools.partial(kernel, p),
        out_shape=(
            jax.ShapeDtypeStruct(q_latent.shape, bf16),
            jax.ShapeDtypeStruct((1, n * p.cap, p.hidden), bf16),
            jax.ShapeDtypeStruct((p.block, p.lat), bf16),
            jax.ShapeDtypeStruct((p.block, p.rope), bf16),
        ),
        in_specs=[smem, smem] + [vmem] * 6 + [hbm] * 4,
        out_specs=(vmem,) * 4,
        scratch_shapes=[
            pltpu.VMEM(q_latent.shape, bf16),
            pltpu.VMEM(q_rope.shape, bf16),
            pltpu.VMEM(gate_weight.shape[1:], bf16),
            pltpu.VMEM(up_weight.shape[1:], bf16),
            pltpu.VMEM((n, p.block, p.kw), bf16),
            pltpu.VMEM((nh, n, p.slot_rows, p.cw), bf16),
            pltpu.VMEM((n, p.slot_rows, p.cw), bf16),
            pltpu.VMEM((p.tok, p.keys), f32),
            pltpu.VMEM((n * p.cap, p.hidden), f32),
            dma((4,)),
            dma((n,)), dma((n,)), dma((n,)), dma((n,)), dma((n,)), dma((n,)),
            dma((p.nx, n)), dma((p.nx, n)), dma((p.nx, n)), dma((p.nx, n)),
        ],
        compiler_params=pltpu.CompilerParams(
            collective_id=0, has_side_effects=True, vmem_limit_bytes=56 * 1024 * 1024),
    )(prefix_len, owners, routes.T, moe_input, prefix_latent, prefix_rope, span_latent, span_rope,
      q_latent, q_rope, gate_weight, up_weight)


def solution(mesh):
    in_specs = (
        P(("group", "expert"), "head"),
        P(("group", "expert"), "head"),
        P(("group", "expert"), None),
        P(("group", "expert"), None),
        P(("group", "expert"), None),
        P(("group", "expert"), None),
        P("group"),
        P(("group", "expert"), "head"),
        P(("group", "expert"), None),
        P("group"),
        P("expert", None, "head"),
        P("expert", None, "head"),
    )
    out_specs = (
        P(("group", "expert"), "head"),
        P(("group", "expert"), None, "head"),
        P(("group", "expert"), None),
        P(("group", "expert"), None),
    )
    return jax.shard_map(body, mesh=mesh, in_specs=in_specs, out_specs=out_specs, check_vma=False)
```

```python
import functools

import jax
import jax.numpy as jnp
from jax import lax
from jax.experimental import pallas as pl
from jax.experimental.pallas import tpu as pltpu
from jax.sharding import PartitionSpec as P

SOFTMAX_SCALE = 192.0 ** (-0.5)
MESH = pl.DeviceIdType.MESH
NT = (((1,), (1,)), ((), ()))
AHEAD = 3
KV_AT = 0
KV_USE = 2


def each(count, step):
    if count <= 4:
        for i in range(count):
            step(i)
    else:
        def one(i, carry):
            step(i)
            return carry
        lax.fori_loop(0, count, one, 0)


def each_from(first, count, step):
    each(count - first, lambda i: step(i + first))


class Plan:
    def __init__(self, n, heads_axis, tok, pre, lat, rope, heads, width, top, hidden):
        self.n, self.nh, self.nx = n, heads_axis, heads_axis // 2
        self.tok, self.pre, self.lat, self.rope, self.heads = tok, pre, lat, rope, heads
        self.block = tok + pre
        self.keys = n * self.block
        self.kw = lat + 2 * rope
        self.width, self.top, self.hidden = width, top, hidden
        self.cap = min(tok, max(2, 9 * tok * top // (8 * n)))
        self.cw = 256 if width % 256 == 0 else 128
        self.chunks = width // self.cw
        self.main = self.cap // 16 * 16
        self.tail = self.cap - self.main
        self.parts = 16 // self.tail if self.tail else 0
        self.per_part = -(-self.chunks // self.parts) if self.tail else 0
        self.slot_rows = self.chunks * self.main + 16 * self.per_part
        self.halves = 2 if self.slot_rows % 32 == 0 else 1
        first = -(-(self.kw // 128) // 2) * 128
        self.cols = (pl.ds(0, first), pl.ds(first, self.kw - first))
        tiles, self.rows, at = self.block // 16, [], 0
        for x in range(self.nx):
            count = tiles // self.nx + (1 if x < tiles % self.nx else 0)
            self.rows.append(pl.ds(at * 16, count * 16) if count else None)
            at += count

    def piece(self, h):
        rows = self.rows[h // 2]
        return None if rows is None else (rows, self.cols[h % 2])


def kernel(
    p,
    limit_ref, owners_ref, routes_ref, feat_ref, prelat_ref, prerope_ref, spanlat_ref, spanrope_ref,
    qlat_hbm, qrope_hbm, gate_hbm, up_hbm,
    att_ref, hidden_ref, miglat_ref, migrope_ref,
    qlat, qrope, gate, up, kv, slots, outgoing, bias, assembled,
    local_sem, kvz_s, kvz_r, kvx_s, kvx_r, kvc_s, kvc_r, sz_s, sz_r, sx_s, sx_r, sc_s, sc_r,
):
    n, nx = p.n, p.nx
    me = lax.axis_index("expert")
    head = lax.axis_index("head")
    core = lax.rem(head, 2)
    xpos = lax.div(head, 2)
    partner = head + 1 - 2 * core

    def z_to(k):
        return lax.rem(me - k + n, n)

    def z_from(k):
        return lax.rem(me + k, n)

    def x_to(j):
        return lax.rem(xpos - j + nx, nx) * 2 + core

    def x_from(j):
        return lax.rem(xpos + j, nx) * 2 + core

    barrier = pltpu.get_barrier_semaphore()
    each_from(1, n, lambda k: pl.semaphore_signal(
        barrier, inc=1, device_id={"expert": z_to(k)}, device_id_type=MESH))
    each_from(1, nx, lambda j: pl.semaphore_signal(
        barrier, inc=1, device_id={"head": x_to(j)}, device_id_type=MESH))
    pl.semaphore_signal(barrier, inc=1, device_id={"head": partner}, device_id_type=MESH)

    loads = [
        pltpu.make_async_copy(src, dst, local_sem.at[i])
        for i, (src, dst) in enumerate(
            ((qlat_hbm, qlat), (qrope_hbm, qrope), (gate_hbm.at[0], gate), (up_hbm.at[0], up)))
    ]
    for load in loads:
        load.start()

    limit = limit_ref[0]
    prefix_pos = me * p.pre + lax.broadcasted_iota(jnp.int32, (p.pre, 1), 0)
    kept = prefix_pos < limit
    zero_pad = jnp.zeros((p.pre, p.rope), jnp.float32)
    kv[me, 0:p.pre, 0:p.lat] = jnp.where(
        kept, prelat_ref[...].astype(jnp.float32), 0.0).astype(jnp.bfloat16)
    kv[me, p.pre:p.block, 0:p.lat] = spanlat_ref[...]
    kv[me, 0:p.pre, p.lat:p.kw] = jnp.concatenate(
        [jnp.where(kept, prerope_ref[...].astype(jnp.float32), 0.0), zero_pad], axis=1
    ).astype(jnp.bfloat16)
    kv[me, p.pre:p.block, p.lat:p.kw] = jnp.concatenate(
        [spanrope_ref[...], jnp.zeros((p.tok, p.rope), jnp.bfloat16)], axis=1)

    feats = feat_ref[...]
    older = (lax.broadcasted_iota(jnp.int32, (p.tok, p.tok), 0)
             <= lax.broadcasted_iota(jnp.int32, (p.tok, p.tok), 1))
    older = older.astype(jnp.float32).astype(jnp.bfloat16)
    sel_rows = p.main + (16 if p.tail else 0)
    row = lax.broadcasted_iota(jnp.int32, (sel_rows, p.tok), 0)
    slot_id = row
    if p.tail:
        for q in range(1, p.parts):
            slot_id = slot_id - jnp.where(row >= p.main + q * p.tail, p.tail, 0)
    slot_id = slot_id.astype(jnp.float32)

    def slot_values(expert, put):
        named = jnp.zeros((1, p.tok), jnp.float32)
        for t in range(p.top):
            named = jnp.maximum(named, (routes_ref[t:t + 1, :] == expert).astype(jnp.float32))
        named8 = jnp.broadcast_to(named, (16, p.tok))
        rank = jnp.dot(named8.astype(jnp.bfloat16), older, preferred_element_type=jnp.float32) - 1.0
        rank = jnp.where(named8 > 0.5, rank, -1.0)[0:1, :]
        chosen = (rank == slot_id).astype(jnp.float32).astype(jnp.bfloat16)
        picked = jnp.dot(chosen, feats, preferred_element_type=jnp.float32)
        for c in range(p.chunks):
            put(c * p.main, p.main,
                picked[0:p.main, c * p.cw:(c + 1) * p.cw].astype(jnp.bfloat16))
        if p.tail:
            trow = lax.broadcasted_iota(jnp.int32, (16, p.cw), 0)
            for part in range(p.per_part):
                value = jnp.zeros((16, p.cw), jnp.float32)
                for q in range(p.parts):
                    c = q * p.per_part + part
                    if c < p.chunks:
                        inside = (trow >= q * p.tail) & (trow < (q + 1) * p.tail)
                        value = jnp.where(
                            inside, picked[p.main:sel_rows, c * p.cw:(c + 1) * p.cw], value)
                put(p.chunks * p.main + 16 * part, 16, value.astype(jnp.bfloat16))

    def fill(k):
        def put(at, rows, value):
            outgoing[k, at:at + rows, :] = value
        slot_values(z_to(k), put)

    def fill_own():
        def put(at, rows, value):
            slots[head, me, at:at + rows, :] = value
        slot_values(me, put)

    def kv_copy(h, k, sems, target):
        rows, cols = p.piece(h)
        ref = kv.at[z_from(k), rows, cols]
        return pltpu.make_async_remote_copy(
            src_ref=ref, dst_ref=ref, send_sem=sems[0], recv_sem=sems[1],
            device_id=target, device_id_type=MESH)

    def kv_z(h, k):
        rows, cols = p.piece(h)
        ref = kv.at[me, rows, cols]
        return pltpu.make_async_remote_copy(
            src_ref=ref, dst_ref=ref, send_sem=kvz_s.at[k], recv_sem=kvz_r.at[k],
            device_id={"expert": z_to(k)}, device_id_type=MESH)

    def kv_z_in(h, k):
        return kv_copy(h, k, (kvz_s.at[k], kvz_r.at[k]), {"expert": z_to(k)})

    def kv_x(h, j, k):
        return kv_copy(h, k, (kvx_s.at[j, k], kvx_r.at[j, k]), {"head": x_to(j)})

    def kv_c(h, j, k):
        return kv_copy(h, k, (kvc_s.at[j, k], kvc_r.at[j, k]), {"head": partner})

    def by_head(step):
        for h in range(p.nh):
            def at(j, c):
                return ((h // 2 + j) % nx) * 2 + c
            along = [(j, at(j, h % 2)) for j in range(1, nx) if p.piece(at(j, 0))]
            across = [(j, at(j, 1 - h % 2)) for j in range(nx) if p.piece(at(j, 0))]
            pl.when(head == h)(functools.partial(step, h, p.piece(h) is not None, along, across))

    part_rows = p.slot_rows // p.halves

    def part_of(i):
        return pl.ds(i * part_rows, part_rows)

    def slot_z(k, i):
        return pltpu.make_async_remote_copy(
            src_ref=outgoing.at[k, part_of(i)], dst_ref=slots.at[head, me, part_of(i)],
            send_sem=sz_s.at[k, i], recv_sem=sz_r.at[k, i],
            device_id={"expert": z_to(k)}, device_id_type=MESH)

    def slot_z_in(k, i):
        return pltpu.make_async_remote_copy(
            src_ref=outgoing.at[k, part_of(i)], dst_ref=slots.at[head, z_from(k), part_of(i)],
            send_sem=sz_s.at[k, i], recv_sem=sz_r.at[k, i],
            device_id={"expert": z_to(k)}, device_id_type=MESH)

    def slot_x(j, k, i, whose):
        ref = slots.at[whose, z_from(k), part_of(i)]
        return pltpu.make_async_remote_copy(
            src_ref=ref, dst_ref=ref, send_sem=sx_s.at[j, k, i], recv_sem=sx_r.at[j, k, i],
            device_id={"head": x_to(j)}, device_id_type=MESH)

    def slot_c(j, k, i, whose):
        ref = slots.at[whose, z_from(k), part_of(i)]
        return pltpu.make_async_remote_copy(
            src_ref=ref, dst_ref=ref, send_sem=sc_s.at[j, k, i], recv_sem=sc_r.at[j, k, i],
            device_id={"head": partner}, device_id_type=MESH)

    def forward_own(k, i):
        each_from(1, nx, lambda j: slot_x(j, k, i, head).start())
        slot_c(0, k, i, head).start()

    def forward_x(k, i):
        def one(j):
            slot_x(j, k, i, x_from(j)).wait_recv()
            slot_c(j, k, i, x_from(j)).start()
        each_from(1, nx, one)

    def each_part(step):
        for i in range(p.halves):
            step(i)

    each_from(1, n, fill)
    fill_own()

    pl.semaphore_wait(barrier, n - 1 + nx - 1 + 1)

    def kv_first(h, own, along, across):
        if own:
            each_from(1, n, lambda k: kv_z(h, k).start())

    def kv_forward(h, own, along, across):
        def one(k):
            kv_z_in(h, k).wait_recv()
            for j in range(1, nx):
                kv_x(h, j, k).start()
            kv_c(h, 0, k).start()
        if own:
            each_from(1, n, one)

    def kv_onward(h, own, along, across):
        def one(k):
            for j, other in along:
                kv_x(other, j, k).wait_recv()
                kv_c(other, j, k).start()
        each_from(1, n, one)

    def kv_take(h, own, along, across):
        def one(k):
            for j, other in across:
                kv_c(other, j, k).wait_recv()
        each_from(1, n, one)

    def kv_sent(h, own, along, across):
        def one(k):
            if own:
                kv_z(h, k).wait_send()
                for j in range(1, nx):
                    kv_x(h, j, k).wait_send()
                kv_c(h, 0, k).wait_send()
            for j, other in along:
                kv_c(other, j, k).wait_send()
        each_from(1, n, one)

    units = [(k, i) for k in range(1, n) for i in range(p.halves)]
    ahead = AHEAD if n <= 4 else len(units)
    if KV_AT == 0:
        by_head(kv_first)
    each_part(lambda i: forward_own(0, i))
    if n <= 4:
        for k, i in units[:ahead]:
            slot_z(k, i).start()
    else:
        each_part(lambda i: each_from(1, n, lambda k: slot_z(k, i).start()))
    if KV_AT == 1:
        by_head(kv_first)

    col = lax.broadcasted_iota(jnp.int32, (p.tok, p.keys), 1).astype(jnp.float32)
    query = (me * p.tok + lax.broadcasted_iota(jnp.int32, (p.tok, p.keys), 0)).astype(jnp.float32)
    source = jnp.floor((col + 0.5) * (1.0 / p.block))
    within = col - source * p.block
    in_prefix = within < p.pre
    reach = jnp.where(in_prefix, limit.astype(jnp.float32) - 1.0, query)
    place = jnp.where(in_prefix, source * p.pre + within, source * p.tok + within - p.pre)
    bias[...] = jnp.where(place <= reach, 0.0, -1e30)


    group = 4 if p.heads % 4 == 0 else 2
    pairs = group // 2

    def attend(g):
        keys = kv[...].reshape(p.keys, p.kw)
        values = keys[:, 0:p.lat]
        rope_even = keys[:, p.lat:p.kw]
        rope_odd = jnp.concatenate([rope_even[:, p.rope:], rope_even[:, :p.rope]], axis=1)
        order = list(range(0, group, 2)) + list(range(1, group, 2))

        def lat_at(h):
            return pl.ds(pl.multiple_of((g * group + h) * p.lat, 128), p.lat)

        q_lat = jnp.concatenate([qlat[:, lat_at(h)] for h in order], axis=0)
        q_rot = jnp.concatenate(
            [qrope[:, pl.ds(pl.multiple_of((g * pairs + i) * 2 * p.rope, 128), 2 * p.rope)]
             for i in range(pairs)], axis=0)
        scores = lax.dot_general(q_lat, values, NT, preferred_element_type=jnp.float32)
        rot = jnp.concatenate(
            [lax.dot_general(q_rot, rope_even, NT, preferred_element_type=jnp.float32),
             lax.dot_general(q_rot, rope_odd, NT, preferred_element_type=jnp.float32)], axis=0)
        shown = (scores + rot) * SOFTMAX_SCALE + jnp.concatenate([bias[...]] * group, axis=0)
        weights = jnp.exp(shown - jnp.max(shown, axis=1, keepdims=True))
        total = jnp.sum(weights, axis=1, keepdims=True)
        mixed = jnp.dot(weights.astype(jnp.bfloat16), values, preferred_element_type=jnp.float32)
        result = (mixed / total).astype(jnp.bfloat16)
        for i, h in enumerate(order):
            att_ref[:, lat_at(h)] = result[i * p.tok:(i + 1) * p.tok, :]

    steps = p.heads // group

    def attend_all(first, last):
        lax.fori_loop(first, last, lambda g, carry: (attend(g), carry)[1], 0)

    def kv_gathered():
        by_head(kv_forward)
        by_head(kv_onward)
        by_head(kv_take)
        loads[0].wait()
        loads[1].wait()

    if n <= 4:
        before = [(0, i) for i in range(p.halves)]
        started = 0
        for at, (k, i) in enumerate(units):
            if at == KV_USE:
                kv_gathered()
                started = at
            slot_z_in(k, i).wait_recv()
            forward_own(k, i)
            if at + ahead < len(units):
                slot_z(*units[at + ahead]).start()
            forward_x(*before[0])
            before = before[1:] + [(k, i)]
            if at >= KV_USE:
                span = len(units) - KV_USE
                first, last = (steps * (at - KV_USE + d) // span for d in (0, 1))
                if last > first:
                    attend_all(first, last)
    else:
        kv_gathered()
        each_part(lambda i: forward_x(0, i))

        def many(k):
            def one(i):
                slot_z_in(k, i).wait_recv()
                forward_own(k, i)
            each_part(one)
        each_from(1, n, many)
        before = [(n - 1, i) for i in range(p.halves)]
        each_part(lambda i: each_from(1, n - 1, lambda k: forward_x(k, i)))
        attend_all(0, steps)

    mine = jnp.int32(0)
    for s in range(n):
        mine = jnp.where(owners_ref[s] == me, s, mine)
    block = kv[mine]
    miglat_ref[...] = block[:, 0:p.lat]
    turned = jnp.transpose(block[:, p.lat:p.kw].astype(jnp.float32))
    migrope_ref[...] = turned[0:p.rope, :].astype(jnp.bfloat16)

    loads[2].wait()
    loads[3].wait()
    rows_main, rows_tail = n * p.main, 16 * n if p.tail else 0
    tail_row = lax.broadcasted_iota(jnp.int32, (n, 16, p.cw), 1)

    def expert_part(which, totals):
        gated, upward = totals
        for c in range(p.chunks):
            lhs = slots[which, :, c * p.main:(c + 1) * p.main, :].reshape(rows_main, p.cw)
            if p.tail:
                q, part = c // p.per_part, c % p.per_part
                at = p.chunks * p.main + 16 * part
                extra = slots[which, :, at:at + 16, :].astype(jnp.float32)
                inside = (tail_row >= q * p.tail) & (tail_row < (q + 1) * p.tail)
                extra = jnp.where(inside, extra, 0.0).astype(jnp.bfloat16)
                lhs = jnp.concatenate([lhs, extra.reshape(rows_tail, p.cw)], axis=0)
            at = pl.ds(pl.multiple_of(which * p.width + c * p.cw, 128), p.cw)
            gated = gated + jnp.dot(lhs, gate[at, :], preferred_element_type=jnp.float32)
            upward = upward + jnp.dot(lhs, up[at, :], preferred_element_type=jnp.float32)
        return gated, upward

    zero = jnp.zeros((rows_main + rows_tail, p.hidden), jnp.float32)
    totals = expert_part(head, (zero, zero))
    each_part(lambda i: each(n, lambda k: slot_c(0, k, i, partner).wait_recv()))
    totals = expert_part(partner, totals)
    for k, i in before:
        forward_x(k, i)
    for j in range(1, nx):
        totals = expert_part(x_from(j), totals)
    for j in range(1, nx):
        whose = x_from(j) + 1 - 2 * core
        each_part(lambda i: each(n, lambda k: slot_c(j, k, i, whose).wait_recv()))
        totals = expert_part(whose, totals)
    gated, upward = totals

    def finish(g, u):
        return g / (1.0 + jnp.exp(-g)) * u

    for s in range(n):
        at = slice(s * p.main, (s + 1) * p.main)
        assembled[s * p.cap:s * p.cap + p.main, :] = finish(gated[at, :], upward[at, :])
        if p.tail:
            g = jnp.zeros((p.tail, p.hidden), jnp.float32)
            u = g
            for q in range(p.parts):
                at = rows_main + 16 * s + q * p.tail
                g = g + gated[at:at + p.tail, :]
                u = u + upward[at:at + p.tail, :]
            assembled[s * p.cap + p.main:(s + 1) * p.cap, :] = finish(g, u)
    hidden_ref[0] = assembled[...].astype(jnp.bfloat16)

    by_head(kv_sent)
    each_part(lambda i: each_from(1, n, lambda k: slot_z(k, i).wait_send()))

    def sent(k):
        def one(i):
            each_from(1, nx, lambda j: slot_x(j, k, i, head).wait_send())
            slot_c(0, k, i, head).wait_send()
            each_from(1, nx, lambda j: slot_c(j, k, i, x_from(j)).wait_send())
        each_part(one)
    each(n, sent)


def place_kernel(count, *refs):
    sources, targets = refs[:count], refs[count:2 * count]
    held, in_sem, out_sem = refs[2 * count:3 * count], refs[3 * count], refs[3 * count + 1]
    ins = [pltpu.make_async_copy(a, b, in_sem.at[i])
           for i, (a, b) in enumerate(zip(sources, held))]
    outs = [pltpu.make_async_copy(a, b, out_sem.at[i])
            for i, (a, b) in enumerate(zip(held, targets))]
    for copy in ins:
        copy.start()
    for i in range(count):
        ins[i].wait()
        outs[i].start()
    for copy in outs:
        copy.wait()


def body(
    q_latent, q_rope, prefix_latent, prefix_rope, span_latent, span_rope,
    prefix_len, moe_input, routes, owners, gate_weight, up_weight,
):
    n = lax.axis_size("expert")
    nh = lax.axis_size("head")
    rope = span_rope.shape[1]
    p = Plan(
        n, nh, span_latent.shape[0], prefix_latent.shape[0], span_latent.shape[1], rope,
        q_rope.shape[1] // rope, moe_input.shape[1], routes.shape[1], gate_weight.shape[2])
    bf16, f32 = jnp.bfloat16, jnp.float32
    vmem = pl.BlockSpec(memory_space=pltpu.VMEM)
    smem = pl.BlockSpec(memory_space=pltpu.SMEM)
    hbm = pl.BlockSpec(memory_space=pl.ANY)
    dma = pltpu.SemaphoreType.DMA
    results = pl.pallas_call(
        functools.partial(kernel, p),
        out_shape=(
            jax.ShapeDtypeStruct(q_latent.shape, bf16),
            jax.ShapeDtypeStruct((1, n * p.cap, p.hidden), bf16),
            jax.ShapeDtypeStruct((p.block, p.lat), bf16),
            jax.ShapeDtypeStruct((p.rope, p.block), bf16),
        ),
        in_specs=[smem, smem] + [vmem] * 6 + [hbm] * 4,
        out_specs=(vmem,) * 4,
        scratch_shapes=[
            pltpu.VMEM(q_latent.shape, bf16),
            pltpu.VMEM(q_rope.shape, bf16),
            pltpu.VMEM(gate_weight.shape[1:], bf16),
            pltpu.VMEM(up_weight.shape[1:], bf16),
            pltpu.VMEM((n, p.block, p.kw), bf16),
            pltpu.VMEM((nh, n, p.slot_rows, p.cw), bf16),
            pltpu.VMEM((n, p.slot_rows, p.cw), bf16),
            pltpu.VMEM((p.tok, p.keys), f32),
            pltpu.VMEM((n * p.cap, p.hidden), f32),
            dma((4,)),
            dma((n,)), dma((n,)), dma((p.nx, n)), dma((p.nx, n)), dma((p.nx, n)), dma((p.nx, n)),
            dma((n, p.halves)), dma((n, p.halves)),
            dma((p.nx, n, p.halves)), dma((p.nx, n, p.halves)),
            dma((p.nx, n, p.halves)), dma((p.nx, n, p.halves)),
        ],
        compiler_params=pltpu.CompilerParams(
            collective_id=0, has_side_effects=True, vmem_limit_bytes=56 * 1024 * 1024),
    )(prefix_len, owners, routes.T, moe_input, prefix_latent, prefix_rope, span_latent, span_rope,
      q_latent, q_rope, gate_weight, up_weight)
    attended, hidden, mig_lat, mig_rope = pl.pallas_call(
        functools.partial(place_kernel, 4),
        out_shape=[jax.ShapeDtypeStruct(r.shape, r.dtype) for r in results],
        in_specs=[hbm] * 4,
        out_specs=[hbm] * 4,
        scratch_shapes=[pltpu.VMEM(r.shape, r.dtype) for r in results] + [dma((4,)), dma((4,))],
    )(*results)
    return attended, hidden, mig_lat, mig_rope.T


def solution(mesh):
    in_specs = (
        P(("group", "expert"), "head"),
        P(("group", "expert"), "head"),
        P(("group", "expert"), None),
        P(("group", "expert"), None),
        P(("group", "expert"), None),
        P(("group", "expert"), None),
        P("group"),
        P(("group", "expert"), "head"),
        P(("group", "expert"), None),
        P("group"),
        P("expert", None, "head"),
        P("expert", None, "head"),
    )
    out_specs = (
        P(("group", "expert"), "head"),
        P(("group", "expert"), None, "head"),
        P(("group", "expert"), None),
        P(("group", "expert"), None),
    )
    return jax.shard_map(body, mesh=mesh, in_specs=in_specs, out_specs=out_specs, check_vma=False)
```

```python
import functools

import jax
import jax.numpy as jnp
from jax import lax
from jax.experimental import pallas as pl
from jax.experimental.pallas import tpu as pltpu
from jax.sharding import PartitionSpec as P

SOFTMAX_SCALE = 192.0 ** (-0.5)
MESH = pl.DeviceIdType.MESH
NT = (((1,), (1,)), ((), ()))
AHEAD = 3
KV_AT = 0
KV_USE = 2


def each(count, step):
    if count <= 4:
        for i in range(count):
            step(i)
    else:
        def one(i, carry):
            step(i)
            return carry
        lax.fori_loop(0, count, one, 0)


def each_from(first, count, step):
    each(count - first, lambda i: step(i + first))


class Plan:
    def __init__(self, n, heads_axis, tok, pre, lat, rope, heads, width, top, hidden):
        self.n, self.nh, self.nx = n, heads_axis, heads_axis // 2
        self.tok, self.pre, self.lat, self.rope, self.heads = tok, pre, lat, rope, heads
        self.block = tok + pre
        self.keys = n * self.block
        self.kw = lat + 2 * rope
        self.width, self.top, self.hidden = width, top, hidden
        self.cap = min(tok, max(2, 9 * tok * top // (8 * n)))
        self.cw = 256 if width % 256 == 0 else 128
        self.chunks = width // self.cw
        self.main = self.cap // 16 * 16
        self.tail = self.cap - self.main
        self.parts = 16 // self.tail if self.tail else 0
        self.per_part = -(-self.chunks // self.parts) if self.tail else 0
        self.slot_rows = self.chunks * self.main + 16 * self.per_part
        self.halves = 2 if self.slot_rows % 32 == 0 else 1
        first = -(-(self.kw // 128) // 2) * 128
        self.cols = (pl.ds(0, first), pl.ds(first, self.kw - first))
        tiles, self.rows, at = self.block // 16, [], 0
        for x in range(self.nx):
            count = tiles // self.nx + (1 if x < tiles % self.nx else 0)
            self.rows.append(pl.ds(at * 16, count * 16) if count else None)
            at += count

    def piece(self, h):
        rows = self.rows[h // 2]
        return None if rows is None else (rows, self.cols[h % 2])


def kernel(
    p,
    limit_ref, owners_ref, routes_ref, feat_ref, prelat_ref, prerope_ref, spanlat_ref, spanrope_ref,
    qlat_hbm, qrope_hbm, gate_hbm, up_hbm,
    att_ref, hidden_ref, miglat_ref, migrope_ref,
    qlat, qrope, gate, up, kv, slots, outgoing, bias, assembled,
    local_sem, kvz_s, kvz_r, kvx_s, kvx_r, kvc_s, kvc_r, sz_s, sz_r, sx_s, sx_r, sc_s, sc_r,
):
    n, nx = p.n, p.nx
    me = lax.axis_index("expert")
    head = lax.axis_index("head")
    core = lax.rem(head, 2)
    xpos = lax.div(head, 2)
    partner = head + 1 - 2 * core

    def z_to(k):
        return lax.rem(me - k + n, n)

    def z_from(k):
        return lax.rem(me + k, n)

    def x_to(j):
        return lax.rem(xpos - j + nx, nx) * 2 + core

    def x_from(j):
        return lax.rem(xpos + j, nx) * 2 + core

    barrier = pltpu.get_barrier_semaphore()
    each_from(1, n, lambda k: pl.semaphore_signal(
        barrier, inc=1, device_id={"expert": z_to(k)}, device_id_type=MESH))
    each_from(1, nx, lambda j: pl.semaphore_signal(
        barrier, inc=1, device_id={"head": x_to(j)}, device_id_type=MESH))
    pl.semaphore_signal(barrier, inc=1, device_id={"head": partner}, device_id_type=MESH)

    loads = [
        pltpu.make_async_copy(src, dst, local_sem.at[i])
        for i, (src, dst) in enumerate(
            ((qlat_hbm, qlat), (qrope_hbm, qrope), (gate_hbm.at[0], gate), (up_hbm.at[0], up)))
    ]
    for load in loads:
        load.start()

    limit = limit_ref[0]
    prefix_pos = me * p.pre + lax.broadcasted_iota(jnp.int32, (p.pre, 1), 0)
    kept = prefix_pos < limit
    zero_pad = jnp.zeros((p.pre, p.rope), jnp.float32)
    kv[me, 0:p.pre, 0:p.lat] = jnp.where(
        kept, prelat_ref[...].astype(jnp.float32), 0.0).astype(jnp.bfloat16)
    kv[me, p.pre:p.block, 0:p.lat] = spanlat_ref[...]
    kv[me, 0:p.pre, p.lat:p.kw] = jnp.concatenate(
        [jnp.where(kept, prerope_ref[...].astype(jnp.float32), 0.0), zero_pad], axis=1
    ).astype(jnp.bfloat16)
    kv[me, p.pre:p.block, p.lat:p.kw] = jnp.concatenate(
        [spanrope_ref[...], jnp.zeros((p.tok, p.rope), jnp.bfloat16)], axis=1)

    feats = feat_ref[...]
    older = (lax.broadcasted_iota(jnp.int32, (p.tok, p.tok), 0)
             <= lax.broadcasted_iota(jnp.int32, (p.tok, p.tok), 1))
    older = older.astype(jnp.float32).astype(jnp.bfloat16)
    sel_rows = p.main + (16 if p.tail else 0)
    row = lax.broadcasted_iota(jnp.int32, (sel_rows, p.tok), 0)
    slot_id = row
    if p.tail:
        for q in range(1, p.parts):
            slot_id = slot_id - jnp.where(row >= p.main + q * p.tail, p.tail, 0)
    slot_id = slot_id.astype(jnp.float32)

    def slot_values(expert, put):
        named = jnp.zeros((1, p.tok), jnp.float32)
        for t in range(p.top):
            named = jnp.maximum(named, (routes_ref[t:t + 1, :] == expert).astype(jnp.float32))
        named8 = jnp.broadcast_to(named, (16, p.tok))
        rank = jnp.dot(named8.astype(jnp.bfloat16), older, preferred_element_type=jnp.float32) - 1.0
        rank = jnp.where(named8 > 0.5, rank, -1.0)[0:1, :]
        chosen = (rank == slot_id).astype(jnp.float32).astype(jnp.bfloat16)
        picked = jnp.dot(chosen, feats, preferred_element_type=jnp.float32)
        for c in range(p.chunks):
            put(c * p.main, p.main,
                picked[0:p.main, c * p.cw:(c + 1) * p.cw].astype(jnp.bfloat16))
        if p.tail:
            trow = lax.broadcasted_iota(jnp.int32, (16, p.cw), 0)
            for part in range(p.per_part):
                value = jnp.zeros((16, p.cw), jnp.float32)
                for q in range(p.parts):
                    c = q * p.per_part + part
                    if c < p.chunks:
                        inside = (trow >= q * p.tail) & (trow < (q + 1) * p.tail)
                        value = jnp.where(
                            inside, picked[p.main:sel_rows, c * p.cw:(c + 1) * p.cw], value)
                put(p.chunks * p.main + 16 * part, 16, value.astype(jnp.bfloat16))

    def fill(k):
        def put(at, rows, value):
            outgoing[k, at:at + rows, :] = value
        slot_values(z_to(k), put)

    def fill_own():
        def put(at, rows, value):
            slots[head, me, at:at + rows, :] = value
        slot_values(me, put)

    def kv_copy(h, k, sems, target):
        rows, cols = p.piece(h)
        ref = kv.at[z_from(k), rows, cols]
        return pltpu.make_async_remote_copy(
            src_ref=ref, dst_ref=ref, send_sem=sems[0], recv_sem=sems[1],
            device_id=target, device_id_type=MESH)

    def kv_z(h, k):
        rows, cols = p.piece(h)
        ref = kv.at[me, rows, cols]
        return pltpu.make_async_remote_copy(
            src_ref=ref, dst_ref=ref, send_sem=kvz_s.at[k], recv_sem=kvz_r.at[k],
            device_id={"expert": z_to(k)}, device_id_type=MESH)

    def kv_z_in(h, k):
        return kv_copy(h, k, (kvz_s.at[k], kvz_r.at[k]), {"expert": z_to(k)})

    def kv_x(h, j, k):
        return kv_copy(h, k, (kvx_s.at[j, k], kvx_r.at[j, k]), {"head": x_to(j)})

    def kv_c(h, j, k):
        return kv_copy(h, k, (kvc_s.at[j, k], kvc_r.at[j, k]), {"head": partner})

    def by_head(step):
        for h in range(p.nh):
            def at(j, c):
                return ((h // 2 + j) % nx) * 2 + c
            along = [(j, at(j, h % 2)) for j in range(1, nx) if p.piece(at(j, 0))]
            across = [(j, at(j, 1 - h % 2)) for j in range(nx) if p.piece(at(j, 0))]
            pl.when(head == h)(functools.partial(step, h, p.piece(h) is not None, along, across))

    part_rows = p.slot_rows // p.halves

    def part_of(i):
        return pl.ds(i * part_rows, part_rows)

    def slot_z(k, i):
        return pltpu.make_async_remote_copy(
            src_ref=outgoing.at[k, part_of(i)], dst_ref=slots.at[head, me, part_of(i)],
            send_sem=sz_s.at[k, i], recv_sem=sz_r.at[k, i],
            device_id={"expert": z_to(k)}, device_id_type=MESH)

    def slot_z_in(k, i):
        return pltpu.make_async_remote_copy(
            src_ref=outgoing.at[k, part_of(i)], dst_ref=slots.at[head, z_from(k), part_of(i)],
            send_sem=sz_s.at[k, i], recv_sem=sz_r.at[k, i],
            device_id={"expert": z_to(k)}, device_id_type=MESH)

    def slot_x(j, k, i, whose):
        ref = slots.at[whose, z_from(k), part_of(i)]
        return pltpu.make_async_remote_copy(
            src_ref=ref, dst_ref=ref, send_sem=sx_s.at[j, k, i], recv_sem=sx_r.at[j, k, i],
            device_id={"head": x_to(j)}, device_id_type=MESH)

    def slot_c(j, k, i, whose):
        ref = slots.at[whose, z_from(k), part_of(i)]
        return pltpu.make_async_remote_copy(
            src_ref=ref, dst_ref=ref, send_sem=sc_s.at[j, k, i], recv_sem=sc_r.at[j, k, i],
            device_id={"head": partner}, device_id_type=MESH)

    def forward_own(k, i):
        each_from(1, nx, lambda j: slot_x(j, k, i, head).start())
        slot_c(0, k, i, head).start()

    def forward_x(k, i):
        def one(j):
            slot_x(j, k, i, x_from(j)).wait_recv()
            slot_c(j, k, i, x_from(j)).start()
        each_from(1, nx, one)

    def each_part(step):
        for i in range(p.halves):
            step(i)

    each_from(1, n, fill)
    fill_own()

    pl.semaphore_wait(barrier, n - 1 + nx - 1 + 1)

    def kv_first(h, own, along, across):
        if own:
            each_from(1, n, lambda k: kv_z(h, k).start())

    def kv_forward(h, own, along, across):
        def one(k):
            kv_z_in(h, k).wait_recv()
            for j in range(1, nx):
                kv_x(h, j, k).start()
            kv_c(h, 0, k).start()
        if own:
            each_from(1, n, one)

    def kv_onward(h, own, along, across):
        def one(k):
            for j, other in along:
                kv_x(other, j, k).wait_recv()
                kv_c(other, j, k).start()
        each_from(1, n, one)

    def kv_take(h, own, along, across):
        def one(k):
            for j, other in across:
                kv_c(other, j, k).wait_recv()
        each_from(1, n, one)

    def kv_sent(h, own, along, across):
        def one(k):
            if own:
                kv_z(h, k).wait_send()
                for j in range(1, nx):
                    kv_x(h, j, k).wait_send()
                kv_c(h, 0, k).wait_send()
            for j, other in along:
                kv_c(other, j, k).wait_send()
        each_from(1, n, one)

    order = list(range(1, n, 2)) + list(range(2, n, 2))
    units = [(k, i) for k in order for i in range(p.halves)]
    ahead = AHEAD if n <= 4 else len(units)
    if KV_AT == 0:
        by_head(kv_first)
    each_part(lambda i: forward_own(0, i))
    if n <= 4:
        for k, i in units[:ahead]:
            slot_z(k, i).start()
    else:
        each_part(lambda i: each_from(1, n, lambda k: slot_z(k, i).start()))
    if KV_AT == 1:
        by_head(kv_first)

    col = lax.broadcasted_iota(jnp.int32, (p.tok, p.keys), 1).astype(jnp.float32)
    query = (me * p.tok + lax.broadcasted_iota(jnp.int32, (p.tok, p.keys), 0)).astype(jnp.float32)
    source = jnp.floor((col + 0.5) * (1.0 / p.block))
    within = col - source * p.block
    in_prefix = within < p.pre
    reach = jnp.where(in_prefix, limit.astype(jnp.float32) - 1.0, query)
    place = jnp.where(in_prefix, source * p.pre + within, source * p.tok + within - p.pre)
    bias[...] = jnp.where(place <= reach, 0.0, -1e30)


    group = 4 if p.heads % 4 == 0 else 2
    pairs = group // 2

    def attend(g):
        keys = kv[...].reshape(p.keys, p.kw)
        values = keys[:, 0:p.lat]
        rope_even = keys[:, p.lat:p.kw]
        rope_odd = jnp.concatenate([rope_even[:, p.rope:], rope_even[:, :p.rope]], axis=1)
        order = list(range(0, group, 2)) + list(range(1, group, 2))

        def lat_at(h):
            return pl.ds(pl.multiple_of((g * group + h) * p.lat, 128), p.lat)

        q_lat = jnp.concatenate([qlat[:, lat_at(h)] for h in order], axis=0)
        q_rot = jnp.concatenate(
            [qrope[:, pl.ds(pl.multiple_of((g * pairs + i) * 2 * p.rope, 128), 2 * p.rope)]
             for i in range(pairs)], axis=0)
        scores = lax.dot_general(q_lat, values, NT, preferred_element_type=jnp.float32)
        rot = jnp.concatenate(
            [lax.dot_general(q_rot, rope_even, NT, preferred_element_type=jnp.float32),
             lax.dot_general(q_rot, rope_odd, NT, preferred_element_type=jnp.float32)], axis=0)
        shown = (scores + rot) * SOFTMAX_SCALE + jnp.concatenate([bias[...]] * group, axis=0)
        weights = jnp.exp(shown - jnp.max(shown, axis=1, keepdims=True))
        total = jnp.sum(weights, axis=1, keepdims=True)
        mixed = jnp.dot(weights.astype(jnp.bfloat16), values, preferred_element_type=jnp.float32)
        result = (mixed / total).astype(jnp.bfloat16)
        for i, h in enumerate(order):
            att_ref[:, lat_at(h)] = result[i * p.tok:(i + 1) * p.tok, :]

    steps = p.heads // group

    def attend_all(first, last):
        lax.fori_loop(first, last, lambda g, carry: (attend(g), carry)[1], 0)

    def kv_gathered():
        by_head(kv_forward)
        by_head(kv_onward)
        by_head(kv_take)
        loads[0].wait()
        loads[1].wait()

    if n <= 4:
        before = [(0, i) for i in range(p.halves)]
        started = 0
        for at, (k, i) in enumerate(units):
            if at == KV_USE:
                kv_gathered()
                started = at
            slot_z_in(k, i).wait_recv()
            forward_own(k, i)
            if at + ahead < len(units):
                slot_z(*units[at + ahead]).start()
            forward_x(*before[0])
            before = before[1:] + [(k, i)]
            if at >= KV_USE:
                span = len(units) - KV_USE
                first, last = (steps * (at - KV_USE + d) // span for d in (0, 1))
                if last > first:
                    attend_all(first, last)
    else:
        kv_gathered()
        each_part(lambda i: forward_x(0, i))

        def many(k):
            def one(i):
                slot_z_in(k, i).wait_recv()
                forward_own(k, i)
            each_part(one)
        each_from(1, n, many)
        before = [(n - 1, i) for i in range(p.halves)]
        each_part(lambda i: each_from(1, n - 1, lambda k: forward_x(k, i)))
        attend_all(0, steps)

    mine = jnp.int32(0)
    for s in range(n):
        mine = jnp.where(owners_ref[s] == me, s, mine)
    block = kv[mine]
    miglat_ref[...] = block[:, 0:p.lat]
    turned = jnp.transpose(block[:, p.lat:p.kw].astype(jnp.float32))
    migrope_ref[...] = turned[0:p.rope, :].astype(jnp.bfloat16)

    loads[2].wait()
    loads[3].wait()
    rows_main, rows_tail = n * p.main, 16 * n if p.tail else 0
    tail_row = lax.broadcasted_iota(jnp.int32, (n, 16, p.cw), 1)

    def expert_part(which, totals):
        gated, upward = totals
        for c in range(p.chunks):
            lhs = slots[which, :, c * p.main:(c + 1) * p.main, :].reshape(rows_main, p.cw)
            if p.tail:
                q, part = c // p.per_part, c % p.per_part
                at = p.chunks * p.main + 16 * part
                extra = slots[which, :, at:at + 16, :].astype(jnp.float32)
                inside = (tail_row >= q * p.tail) & (tail_row < (q + 1) * p.tail)
                extra = jnp.where(inside, extra, 0.0).astype(jnp.bfloat16)
                lhs = jnp.concatenate([lhs, extra.reshape(rows_tail, p.cw)], axis=0)
            at = pl.ds(pl.multiple_of(which * p.width + c * p.cw, 128), p.cw)
            gated = gated + jnp.dot(lhs, gate[at, :], preferred_element_type=jnp.float32)
            upward = upward + jnp.dot(lhs, up[at, :], preferred_element_type=jnp.float32)
        return gated, upward

    zero = jnp.zeros((rows_main + rows_tail, p.hidden), jnp.float32)
    totals = expert_part(head, (zero, zero))
    each_part(lambda i: each(n, lambda k: slot_c(0, k, i, partner).wait_recv()))
    totals = expert_part(partner, totals)
    for k, i in before:
        forward_x(k, i)
    for j in range(1, nx):
        totals = expert_part(x_from(j), totals)
    for j in range(1, nx):
        whose = x_from(j) + 1 - 2 * core
        each_part(lambda i: each(n, lambda k: slot_c(j, k, i, whose).wait_recv()))
        totals = expert_part(whose, totals)
    gated, upward = totals

    def finish(g, u):
        return g / (1.0 + jnp.exp(-g)) * u

    for s in range(n):
        at = slice(s * p.main, (s + 1) * p.main)
        assembled[s * p.cap:s * p.cap + p.main, :] = finish(gated[at, :], upward[at, :])
        if p.tail:
            g = jnp.zeros((p.tail, p.hidden), jnp.float32)
            u = g
            for q in range(p.parts):
                at = rows_main + 16 * s + q * p.tail
                g = g + gated[at:at + p.tail, :]
                u = u + upward[at:at + p.tail, :]
            assembled[s * p.cap + p.main:(s + 1) * p.cap, :] = finish(g, u)
    hidden_ref[0] = assembled[...].astype(jnp.bfloat16)

    by_head(kv_sent)
    each_part(lambda i: each_from(1, n, lambda k: slot_z(k, i).wait_send()))

    def sent(k):
        def one(i):
            each_from(1, nx, lambda j: slot_x(j, k, i, head).wait_send())
            slot_c(0, k, i, head).wait_send()
            each_from(1, nx, lambda j: slot_c(j, k, i, x_from(j)).wait_send())
        each_part(one)
    each(n, sent)


def place_kernel(count, *refs):
    sources, targets = refs[:count], refs[count:2 * count]
    held, in_sem, out_sem = refs[2 * count:3 * count], refs[3 * count], refs[3 * count + 1]
    ins = [pltpu.make_async_copy(a, b, in_sem.at[i])
           for i, (a, b) in enumerate(zip(sources, held))]
    outs = [pltpu.make_async_copy(a, b, out_sem.at[i])
            for i, (a, b) in enumerate(zip(held, targets))]
    for copy in ins:
        copy.start()
    for i in range(count):
        ins[i].wait()
        outs[i].start()
    for copy in outs:
        copy.wait()


def body(
    q_latent, q_rope, prefix_latent, prefix_rope, span_latent, span_rope,
    prefix_len, moe_input, routes, owners, gate_weight, up_weight,
):
    n = lax.axis_size("expert")
    nh = lax.axis_size("head")
    rope = span_rope.shape[1]
    p = Plan(
        n, nh, span_latent.shape[0], prefix_latent.shape[0], span_latent.shape[1], rope,
        q_rope.shape[1] // rope, moe_input.shape[1], routes.shape[1], gate_weight.shape[2])
    bf16, f32 = jnp.bfloat16, jnp.float32
    vmem = pl.BlockSpec(memory_space=pltpu.VMEM)
    smem = pl.BlockSpec(memory_space=pltpu.SMEM)
    hbm = pl.BlockSpec(memory_space=pl.ANY)
    dma = pltpu.SemaphoreType.DMA
    results = pl.pallas_call(
        functools.partial(kernel, p),
        out_shape=(
            jax.ShapeDtypeStruct(q_latent.shape, bf16),
            jax.ShapeDtypeStruct((1, n * p.cap, p.hidden), bf16),
            jax.ShapeDtypeStruct((p.block, p.lat), bf16),
            jax.ShapeDtypeStruct((p.rope, p.block), bf16),
        ),
        in_specs=[smem, smem] + [vmem] * 6 + [hbm] * 4,
        out_specs=(vmem,) * 4,
        scratch_shapes=[
            pltpu.VMEM(q_latent.shape, bf16),
            pltpu.VMEM(q_rope.shape, bf16),
            pltpu.VMEM(gate_weight.shape[1:], bf16),
            pltpu.VMEM(up_weight.shape[1:], bf16),
            pltpu.VMEM((n, p.block, p.kw), bf16),
            pltpu.VMEM((nh, n, p.slot_rows, p.cw), bf16),
            pltpu.VMEM((n, p.slot_rows, p.cw), bf16),
            pltpu.VMEM((p.tok, p.keys), f32),
            pltpu.VMEM((n * p.cap, p.hidden), f32),
            dma((4,)),
            dma((n,)), dma((n,)), dma((p.nx, n)), dma((p.nx, n)), dma((p.nx, n)), dma((p.nx, n)),
            dma((n, p.halves)), dma((n, p.halves)),
            dma((p.nx, n, p.halves)), dma((p.nx, n, p.halves)),
            dma((p.nx, n, p.halves)), dma((p.nx, n, p.halves)),
        ],
        compiler_params=pltpu.CompilerParams(
            collective_id=0, has_side_effects=True, vmem_limit_bytes=56 * 1024 * 1024),
    )(prefix_len, owners, routes.T, moe_input, prefix_latent, prefix_rope, span_latent, span_rope,
      q_latent, q_rope, gate_weight, up_weight)
    attended, hidden, mig_lat, mig_rope = pl.pallas_call(
        functools.partial(place_kernel, 4),
        out_shape=[jax.ShapeDtypeStruct(r.shape, r.dtype) for r in results],
        in_specs=[hbm] * 4,
        out_specs=[hbm] * 4,
        scratch_shapes=[pltpu.VMEM(r.shape, r.dtype) for r in results] + [dma((4,)), dma((4,))],
    )(*results)
    return attended, hidden, mig_lat, mig_rope.T


def solution(mesh):
    in_specs = (
        P(("group", "expert"), "head"),
        P(("group", "expert"), "head"),
        P(("group", "expert"), None),
        P(("group", "expert"), None),
        P(("group", "expert"), None),
        P(("group", "expert"), None),
        P("group"),
        P(("group", "expert"), "head"),
        P(("group", "expert"), None),
        P("group"),
        P("expert", None, "head"),
        P("expert", None, "head"),
    )
    out_specs = (
        P(("group", "expert"), "head"),
        P(("group", "expert"), None, "head"),
        P(("group", "expert"), None),
        P(("group", "expert"), None),
    )
    return jax.shard_map(body, mesh=mesh, in_specs=in_specs, out_specs=out_specs, check_vma=False)
```
